32 devices in a mesh: cohort: 2 (over x), ind: 16 (over z, y, core).
Axes of the slice: x: 2, y: 2, z: 4, core: 2. Of those that a mesh axis runs over, the one named last changes fastest.
Arguments:
- genotypes: float32 [65536, 1200], P(('cohort', 'ind')), parts along dimension 0, may hold values from -6.5 to 6.5
- solution: float32 [16, 65536], P(None, ('cohort', 'ind')), parts along dimension 1, may hold values from -6 to 6
- residual: float32 [16, 65536], P(None, ('cohort', 'ind')), parts along dimension 1, may hold values from -6 to 6
- direction: float32 [16, 65536], P(None, ('cohort', 'ind')), parts along dimension 1, may hold values from -6 to 6
- ratio: float32 [32], P('cohort'), parts along dimension 0, may hold values from 0.2 to 5
Outputs:
- solution_out: float32 [16, 65536], P(None, ('cohort', 'ind')), parts along dimension 1
- residual_out: float32 [16, 65536], P(None, ('cohort', 'ind')), parts along dimension 1
- direction_out: float32 [16, 65536], P(None, ('cohort', 'ind')), parts along dimension 1
The draws below stay inside these ranges and needn't reach their ends.
There are 2 independent parts, one for each index of `cohort`. The reference program is written for one: setup_inputs(seed, part) draws one part's arguments, and reference() takes and returns one part's arrays. A program takes and returns all parts, laid end to end along the dimension named above; each array names one. Nothing has to cross between parts.
All inputs are finite; a program needn't handle non-finite values.
Results may differ from the reference program's by a relative error of at most 0.0003.
Values sent between devices are 32-bit elements; how exact they have to be, the bound alone decides.
A program may use at most 64 MiB of HBM per device.

```python
import math
import jax
import jax.numpy as jnp
from jax import lax

SNPS = 1200
TRAITS = 16
ITERS = 8
PEOPLE = 32768


def draw_genotypes(key, part):
    key = jax.random.fold_in(key, 11)
    key_rate, key_shared, key_own = jax.random.split(key, 3)
    block_count = SNPS // 16
    looseness = jnp.exp(jax.random.uniform(key_rate, (block_count,), minval=math.log(0.05), maxval=math.log(0.7)))
    shared_factor = jnp.clip(jax.random.normal(key_shared, (PEOPLE, block_count)), -4.5, 4.5)
    own_noise = jnp.clip(jax.random.normal(key_own, (PEOPLE, SNPS)), -4.5, 4.5)
    block_of = jnp.arange(SNPS, dtype=jnp.int32) // 16
    column_loose = looseness[block_of]
    values = jnp.sqrt(1.0 - column_loose)[None, :] * shared_factor[:, block_of] + jnp.sqrt(column_loose)[None, :] * own_noise
    return values.astype(jnp.float32)


def block_levels(rng, shape, cuts, least, high):
    loudness = 1.0
    for dim, blocks in cuts:
        draws = jax.random.uniform(jax.random.fold_in(jax.random.fold_in(rng, 6), dim), (blocks,), jnp.float32, least / len(cuts), high / len(cuts))
        loudness = loudness * jnp.repeat(jnp.exp(draws), shape[dim] // blocks).reshape((-1,) + (1,) * (len(shape) - 1 - dim))
    return loudness


def centred(stream_key, shape, width, limit, cuts=(), kind=jnp.bfloat16):
    result = width * jax.random.normal(stream_key, shape, jnp.float32)
    if cuts:
        result = result * block_levels(stream_key, shape, cuts, -0.22, 0.18)
    return jnp.clip(result, -limit, limit).astype(kind)


def setup_inputs(seed: int = 0, part: int = 0) -> dict:
    key_list = jax.random.split(jax.random.key(seed), 6)
    part_keys = jax.random.split(jax.random.fold_in(key_list[5], part), 6)
    genotypes = draw_genotypes(jax.random.fold_in(jax.random.fold_in(key_list[5], part), 71), part)
    solution = centred(part_keys[1], (TRAITS, PEOPLE), 1.0, 6.0, ((1, 16),), jnp.float32)
    residual = centred(part_keys[2], (TRAITS, PEOPLE), 1.0, 6.0, ((1, 16),), jnp.float32)
    direction = centred(part_keys[3], (TRAITS, PEOPLE), 1.0, 6.0, ((1, 16),), jnp.float32)
    ratio = jnp.clip(jnp.exp(jax.random.uniform(part_keys[4], (TRAITS,), jnp.float32, math.log(0.2), math.log(5.0))), 0.2, 5.0)
    return dict(genotypes=genotypes, solution=solution, residual=residual, direction=direction, ratio=ratio)


def apply_operator(direction, genotypes, ratio):
    snp_sums = jnp.dot(direction, genotypes, precision=lax.Precision.HIGHEST, preferred_element_type=jnp.float32)
    back = lax.dot_general(snp_sums, genotypes, (((1,), (1,)), ((), ())), precision=lax.Precision.HIGHEST, preferred_element_type=jnp.float32)
    return back / SNPS + ratio[:, None] * direction


def reference(genotypes, solution, residual, direction, ratio):
    norm_now = jnp.sum(residual * residual, axis=1)
    for step in range(ITERS):
        image = apply_operator(direction, genotypes, ratio)
        alpha = norm_now / jnp.sum(direction * image, axis=1)
        solution = solution + alpha[:, None] * direction
        residual = residual - alpha[:, None] * image
        fresh = jnp.sum(residual * residual, axis=1)
        direction = residual + (fresh / norm_now)[:, None] * direction
        norm_now = fresh
    return solution, residual, direction
```

```python
import functools

import jax
import jax.numpy as jnp
from jax import lax
from jax.experimental import pallas as pl
from jax.experimental.pallas import tpu as pltpu
from jax.sharding import PartitionSpec as P

ITERS = 8
LANES = 128
F32 = jnp.float32
BF16 = jnp.bfloat16


def split(value):
    high = value.astype(BF16)
    low = (value - high.astype(F32)).astype(BF16)
    return high, low


def product(rows, w_high, w_low, transposed=False):
    dims = (((1,), (1 if transposed else 0,)), ((), ()))
    count = rows.shape[0]
    high, low = split(rows)
    both = lax.dot_general(
        jnp.concatenate([high, low], axis=0), w_high, dims, preferred_element_type=F32
    )
    rest = lax.dot_general(high, w_low, dims, preferred_element_type=F32)
    return both[:count] + both[count:] + rest


def cg_kernel(
    n, snps, chunks,
    gh, gl, kh, kl, x_in, r_in, p_in, ratio_in,
    x_out, r_out, p_out,
    part0, rs0, ag0, part, rs, ag, sums_ref, u_ref, image_ref,
    rs_send, rs_recv, ag_send, ag_recv,
):
    me = lax.axis_index("ind")
    people = x_in.shape[1]
    traits = x_in.shape[0]
    owners = [(c * n) // chunks for c in range(chunks)]
    mine = (me * chunks + n - 1) // n
    is_owner = jnp.logical_and((mine * n) // chunks == me, mine < chunks)
    mine = jnp.minimum(mine, chunks - 1)

    barrier = pltpu.get_barrier_semaphore()

    @pl.when(is_owner)
    def _():
        @pl.loop(1, n)
        def _(j):
            pl.semaphore_signal(
                barrier, inc=1, device_id={"ind": lax.rem(me + j, n)},
                device_id_type=pl.DeviceIdType.MESH,
            )

        pl.semaphore_wait(barrier, n - 1)

    @pl.when(jnp.logical_not(is_owner))
    def _():
        for o in owners:
            pl.semaphore_signal(
                barrier, inc=1, device_id={"ind": o},
                device_id_type=pl.DeviceIdType.MESH,
            )
        pl.semaphore_wait(barrier, chunks)

    def scatter_start(src, dst, which):
        for c, o in enumerate(owners):
            @pl.when(me != o)
            def _():
                pltpu.make_async_remote_copy(
                    src_ref=src.at[c], dst_ref=dst.at[lax.rem(me - o - 1 + n, n)],
                    send_sem=rs_send.at[which], recv_sem=rs_recv.at[which],
                    device_id={"ind": o}, device_id_type=pl.DeviceIdType.MESH,
                ).start()

    def local(src, dst, send, recv):
        return pltpu.make_async_remote_copy(
            src_ref=src, dst_ref=dst, send_sem=send, recv_sem=recv,
            device_id={"ind": lax.rem(me + 1, n)},
            device_id_type=pl.DeviceIdType.MESH,
        )

    def sum_and_gather(src, buf, out, which):
        @pl.when(is_owner)
        def _():
            local(buf, buf, rs_send.at[which], rs_recv.at[which]).wait_recv()
            out[mine] = src[mine] + jnp.sum(buf[...], axis=0)

            @pl.loop(1, n)
            def _(j):
                pltpu.make_async_remote_copy(
                    src_ref=out.at[mine], dst_ref=out.at[mine],
                    send_sem=ag_send.at[which], recv_sem=ag_recv.at[which],
                    device_id={"ind": lax.rem(me + j, n)},
                    device_id_type=pl.DeviceIdType.MESH,
                ).start()

    def finish(src, buf, out, which):
        @pl.when(is_owner)
        def _():
            few = out.at[pl.ds(0, chunks - 1)]
            local(few, few, ag_send.at[which], ag_recv.at[which]).wait_recv()
            few = src.at[pl.ds(0, chunks - 1)]
            local(few, few, rs_send.at[which], rs_recv.at[which]).wait_send()
            local(buf, buf, ag_send.at[which], ag_recv.at[which]).wait_send()

        @pl.when(jnp.logical_not(is_owner))
        def _():
            local(out, out, ag_send.at[which], ag_recv.at[which]).wait_recv()
            local(src, src, rs_send.at[which], rs_recv.at[which]).wait_send()

    def put(dst, value):
        for c in range(chunks):
            dst[c] = value[:, c * LANES:(c + 1) * LANES]

    def whole(src):
        return jnp.concatenate([src[c] for c in range(chunks)], axis=1)

    wide = lax.broadcasted_iota(jnp.int32, (1, chunks * LANES), 1)
    real = wide < snps

    put(part0, product(jnp.concatenate([p_in[...], r_in[...]], axis=0), gh[...], gl[...]))
    scatter_start(part0, rs0, 0)
    x_out[...] = x_in[...]
    r_out[...] = r_in[...]
    p_out[...] = p_in[...]
    sum_and_gather(part0, rs0, ag0, 0)
    finish(part0, rs0, ag0, 0)
    start = whole(ag0)
    sums_ref[...] = start[:traits]
    u_ref[...] = start[traits:]
    ratio = ratio_in[...]
    scale = 1.0 / snps
    half = people // 2

    def image_half(s, i):
        cut = pl.ds(i * half, half)
        image_ref[:, cut] = (
            product(s, gh[cut, :], gl[cut, :], True) / snps + ratio * p_out[:, cut]
        )

    @pl.loop(0, ITERS)
    def _(step):
        s = sums_ref[...]
        t = product(s, kh[...], kl[...])
        r, p = r_out[...], p_out[...]
        rr = jnp.sum(r * r, axis=1, keepdims=True)
        rp = jnp.sum(r * p, axis=1, keepdims=True)
        pp = jnp.sum(p * p, axis=1, keepdims=True)
        t = t + jnp.where(
            wide == snps, rr,
            jnp.where(wide == snps + 1, rp, jnp.where(wide == snps + 2, pp, 0.0)),
        )
        put(part, t)
        scatter_start(part, rs, 1)
        image_half(s, 0)
        sum_and_gather(part, rs, ag, 1)
        image_half(s, 1)
        finish(part, rs, ag, 1)

        t = whole(ag)
        rr = t[:, snps:snps + 1]
        rp = t[:, snps + 1:snps + 2]
        pp = t[:, snps + 2:snps + 3]
        t = jnp.where(real, t, 0.0)
        u = u_ref[...]
        ss = jnp.sum(s * s, axis=1, keepdims=True) * scale
        us = jnp.sum(u * s, axis=1, keepdims=True) * scale
        ts = jnp.sum(t * s, axis=1, keepdims=True) * (scale * scale)
        alpha = rr / (ss + ratio * pp)
        cross = us + ratio * rp
        norm = ts + ratio * (2.0 * ss + ratio * pp)
        fresh = rr - alpha * (2.0 * cross - alpha * norm)
        beta = fresh / rr
        u = u - alpha * (t * scale + ratio * s)
        u_ref[...] = u
        sums_ref[...] = u + beta * s
        p = p_out[...]
        x_out[...] = x_out[...] + alpha * p
        r = r_out[...] - alpha * image_ref[...]
        r_out[...] = r
        p_out[...] = r + beta * p


def per_device(n, genotypes, solution, residual, direction, ratio):
    people, snps = genotypes.shape
    traits = solution.shape[0]
    chunks = -(-(snps + 3) // LANES)
    padded = chunks * LANES
    g = jnp.pad(genotypes, ((0, 0), (0, padded - snps)))
    high = lax.reduce_precision(g, 8, 7)
    gh = high.astype(BF16)
    gl = (g - high).astype(BF16)
    dims = (((0,), (0,)), ((), ()))
    hh = lax.dot_general(gh, gh, dims, preferred_element_type=F32)
    hl = lax.dot_general(gh, gl, dims, preferred_element_type=F32)
    gram = hh + hl + hl.T
    k_high = lax.reduce_precision(gram, 8, 7)
    kh = k_high.astype(BF16)
    kl = (gram - k_high).astype(BF16)

    vmem = pl.BlockSpec(memory_space=pltpu.VMEM)
    shape = jax.ShapeDtypeStruct((traits, people), F32)
    return pl.pallas_call(
        functools.partial(cg_kernel, n, snps, chunks),
        out_shape=(shape, shape, shape),
        in_specs=[vmem] * 8,
        out_specs=(vmem, vmem, vmem),
        scratch_shapes=[
            pltpu.VMEM((chunks, 2 * traits, LANES), F32),
            pltpu.VMEM((n - 1, 2 * traits, LANES), F32),
            pltpu.VMEM((chunks, 2 * traits, LANES), F32),
            pltpu.VMEM((chunks, traits, LANES), F32),
            pltpu.VMEM((n - 1, traits, LANES), F32),
            pltpu.VMEM((chunks, traits, LANES), F32),
            pltpu.VMEM((traits, padded), F32),
            pltpu.VMEM((traits, padded), F32),
            pltpu.VMEM((traits, people), F32),
            pltpu.SemaphoreType.DMA((2,)),
            pltpu.SemaphoreType.DMA((2,)),
            pltpu.SemaphoreType.DMA((2,)),
            pltpu.SemaphoreType.DMA((2,)),
        ],
        compiler_params=pltpu.CompilerParams(
            collective_id=0, has_side_effects=True, vmem_limit_bytes=56 * 2**20
        ),
    )(gh, gl, kh, kl, solution, residual, direction, ratio[:, None])


def solution(mesh):
    cols = P(None, ("cohort", "ind"))
    return jax.shard_map(
        functools.partial(per_device, mesh.shape["ind"]),
        mesh=mesh,
        in_specs=(P(("cohort", "ind"), None), cols, cols, cols, P("cohort")),
        out_specs=(cols, cols, cols),
        check_vma=False,
    )
```

```python
import functools

import jax
import jax.numpy as jnp
from jax import lax
from jax.experimental import pallas as pl
from jax.experimental.pallas import tpu as pltpu
from jax.sharding import PartitionSpec as P

ITERS = 8
LANES = 128
ROWS = 256
F32 = jnp.float32
BF16 = jnp.bfloat16


def split(value):
    high = value.astype(BF16)
    low = (value - high.astype(F32)).astype(BF16)
    return high, low


def product(rows, w_high, w_low):
    dims = (((1,), (0,)), ((), ()))
    count = rows.shape[0]
    high, low = split(rows)
    both = lax.dot_general(
        jnp.concatenate([high, low], axis=0), w_high, dims, preferred_element_type=F32
    )
    rest = lax.dot_general(high, w_low, dims, preferred_element_type=F32)
    return both[:count] + both[count:] + rest


def cg_kernel(
    n, snps, chunks,
    g_in, x_in, r_in, p_in, ratio_in,
    x_out, r_out, p_out,
    raw, gh, gl, th, tl, kh, kl, g_sem, first, part0, rs0, ag0, part, rs, ag, sums_ref, u_ref, image_ref,
    rs_send, rs_recv, ag_send, ag_recv,
):
    me = lax.axis_index("ind")
    people = x_in.shape[1]
    traits = x_in.shape[0]
    owners = [(c * n) // chunks for c in range(chunks)]
    mine = (me * chunks + n - 1) // n
    is_owner = jnp.logical_and((mine * n) // chunks == me, mine < chunks)
    mine = jnp.minimum(mine, chunks - 1)

    rows = ROWS if people % ROWS == 0 else people
    steps = people // rows
    tail = (chunks - 1) * LANES

    def load(i):
        cut = pl.ds(pl.multiple_of(i * rows, rows), rows)
        return pltpu.make_async_copy(g_in.at[cut], raw.at[cut], g_sem.at[i])

    for i in range(steps):
        load(i).start()

    barrier = pltpu.get_barrier_semaphore()

    @pl.when(is_owner)
    def _():
        @pl.loop(1, n)
        def _(j):
            pl.semaphore_signal(
                barrier, inc=1, device_id={"ind": lax.rem(me + j, n)},
                device_id_type=pl.DeviceIdType.MESH,
            )

        pl.semaphore_wait(barrier, n - 1)

    @pl.when(jnp.logical_not(is_owner))
    def _():
        for o in owners:
            pl.semaphore_signal(
                barrier, inc=1, device_id={"ind": o},
                device_id_type=pl.DeviceIdType.MESH,
            )
        pl.semaphore_wait(barrier, chunks)

    def scatter_start(src, dst, which):
        for c, o in enumerate(owners):
            @pl.when(me != o)
            def _():
                pltpu.make_async_remote_copy(
                    src_ref=src.at[c], dst_ref=dst.at[lax.rem(me - o - 1 + n, n)],
                    send_sem=rs_send.at[which], recv_sem=rs_recv.at[which],
                    device_id={"ind": o}, device_id_type=pl.DeviceIdType.MESH,
                ).start()

    def local(src, dst, send, recv):
        return pltpu.make_async_remote_copy(
            src_ref=src, dst_ref=dst, send_sem=send, recv_sem=recv,
            device_id={"ind": lax.rem(me + 1, n)},
            device_id_type=pl.DeviceIdType.MESH,
        )

    def sum_and_gather(src, buf, out, which):
        @pl.when(is_owner)
        def _():
            local(buf, buf, rs_send.at[which], rs_recv.at[which]).wait_recv()
            out[mine] = src[mine] + jnp.sum(buf[...], axis=0)

            @pl.loop(1, n)
            def _(j):
                pltpu.make_async_remote_copy(
                    src_ref=out.at[mine], dst_ref=out.at[mine],
                    send_sem=ag_send.at[which], recv_sem=ag_recv.at[which],
                    device_id={"ind": lax.rem(me + j, n)},
                    device_id_type=pl.DeviceIdType.MESH,
                ).start()

    def finish(src, buf, out, which):
        @pl.when(is_owner)
        def _():
            few = out.at[pl.ds(0, chunks - 1)]
            local(few, few, ag_send.at[which], ag_recv.at[which]).wait_recv()
            few = src.at[pl.ds(0, chunks - 1)]
            local(few, few, rs_send.at[which], rs_recv.at[which]).wait_send()
            local(buf, buf, ag_send.at[which], ag_recv.at[which]).wait_send()

        @pl.when(jnp.logical_not(is_owner))
        def _():
            local(out, out, ag_send.at[which], ag_recv.at[which]).wait_recv()
            local(src, src, rs_send.at[which], rs_recv.at[which]).wait_send()

    def put(dst, value):
        for c in range(chunks):
            dst[c] = value[:, c * LANES:(c + 1) * LANES]

    def whole(src):
        return jnp.concatenate([src[c] for c in range(chunks)], axis=1)

    wide = lax.broadcasted_iota(jnp.int32, (1, chunks * LANES), 1)
    real = wide < snps

    gh[:, tail:] = jnp.zeros((people, LANES), BF16)
    gl[:, tail:] = jnp.zeros((people, LANES), BF16)
    first[...] = jnp.zeros_like(first)

    @pl.loop(0, steps)
    def _(i):
        load(i).wait()
        cut = pl.ds(pl.multiple_of(i * rows, rows), rows)
        for c in range(chunks):
            lanes = slice(c * LANES, min((c + 1) * LANES, snps))
            high, low = split(raw[cut, lanes])
            gh[cut, lanes] = high
            gl[cut, lanes] = low
        both = jnp.concatenate([p_in[:, cut], r_in[:, cut]], axis=0)
        first[...] += product(both, gh[cut, :], gl[cut, :])

    put(part0, first[...])
    scatter_start(part0, rs0, 0)
    x_out[...] = x_in[...]
    r_out[...] = r_in[...]
    p_out[...] = p_in[...]

    @pl.loop(0, steps)
    def _(i):
        cut = pl.ds(pl.multiple_of(i * rows, rows), rows)
        th[:, cut] = gh[cut, :].T
        tl[:, cut] = gl[cut, :].T

    sum_and_gather(part0, rs0, ag0, 0)

    width = 2 * LANES
    for j in range(chunks // 2):
        lanes = slice(j * width, (j + 1) * width)
        top = (j + 1) * width
        block = (
            jnp.dot(th[:top], gh[:, lanes], preferred_element_type=F32)
            + jnp.dot(th[:top], gl[:, lanes], preferred_element_type=F32)
            + jnp.dot(tl[:top], gh[:, lanes], preferred_element_type=F32)
        )
        high, low = split(block)
        kh[:top, lanes] = high
        kl[:top, lanes] = low
        for i in range(j):
            under = slice(i * width, (i + 1) * width)
            kh[lanes, under] = high[under].T
            kl[lanes, under] = low[under].T

    finish(part0, rs0, ag0, 0)
    start = whole(ag0)
    sums_ref[...] = start[:traits]
    u_ref[...] = start[traits:]
    ratio = ratio_in[...]
    scale = 1.0 / snps
    half = people // 2

    def image_half(s, i):
        cut = pl.ds(i * half, half)
        image_ref[:, cut] = (
            product(s, th[:, cut], tl[:, cut]) * scale + ratio * p_out[:, cut]
        )

    @pl.loop(0, ITERS)
    def _(step):
        s = sums_ref[...]
        t = product(s, kh[...], kl[...])
        r, p = r_out[...], p_out[...]
        rr = jnp.sum(r * r, axis=1, keepdims=True)
        rp = jnp.sum(r * p, axis=1, keepdims=True)
        pp = jnp.sum(p * p, axis=1, keepdims=True)
        t = t + jnp.where(
            wide == snps, rr,
            jnp.where(wide == snps + 1, rp, jnp.where(wide == snps + 2, pp, 0.0)),
        )
        put(part, t)
        scatter_start(part, rs, 1)
        image_half(s, 0)
        sum_and_gather(part, rs, ag, 1)
        image_half(s, 1)
        finish(part, rs, ag, 1)

        t = whole(ag)
        rr = t[:, snps:snps + 1]
        rp = t[:, snps + 1:snps + 2]
        pp = t[:, snps + 2:snps + 3]
        t = jnp.where(real, t, 0.0)
        u = u_ref[...]
        ss = jnp.sum(s * s, axis=1, keepdims=True) * scale
        us = jnp.sum(u * s, axis=1, keepdims=True) * scale
        ts = jnp.sum(t * s, axis=1, keepdims=True) * (scale * scale)
        alpha = rr / (ss + ratio * pp)
        cross = us + ratio * rp
        norm = ts + ratio * (2.0 * ss + ratio * pp)
        fresh = rr - alpha * (2.0 * cross - alpha * norm)
        beta = fresh / rr
        u = u - alpha * (t * scale + ratio * s)
        u_ref[...] = u
        sums_ref[...] = u + beta * s
        p = p_out[...]
        x_out[...] = x_out[...] + alpha * p
        r = r_out[...] - alpha * image_ref[...]
        r_out[...] = r
        p_out[...] = r + beta * p


def per_device(n, genotypes, solution, residual, direction, ratio):
    people, snps = genotypes.shape
    traits = solution.shape[0]
    chunks = -(-(snps + 3) // LANES)
    chunks += chunks % 2
    padded = chunks * LANES
    rows = ROWS if people % ROWS == 0 else people

    vmem = pl.BlockSpec(memory_space=pltpu.VMEM)
    shape = jax.ShapeDtypeStruct((traits, people), F32)
    return pl.pallas_call(
        functools.partial(cg_kernel, n, snps, chunks),
        out_shape=(shape, shape, shape),
        in_specs=[pl.BlockSpec(memory_space=pl.ANY)] + [vmem] * 4,
        out_specs=(vmem, vmem, vmem),
        scratch_shapes=[
            pltpu.VMEM((people, snps), F32),
            pltpu.VMEM((people, padded), BF16),
            pltpu.VMEM((people, padded), BF16),
            pltpu.VMEM((padded, people), BF16),
            pltpu.VMEM((padded, people), BF16),
            pltpu.VMEM((padded, padded), BF16),
            pltpu.VMEM((padded, padded), BF16),
            pltpu.SemaphoreType.DMA((people // rows,)),
            pltpu.VMEM((2 * traits, padded), F32),
            pltpu.VMEM((chunks, 2 * traits, LANES), F32),
            pltpu.VMEM((n - 1, 2 * traits, LANES), F32),
            pltpu.VMEM((chunks, 2 * traits, LANES), F32),
            pltpu.VMEM((chunks, traits, LANES), F32),
            pltpu.VMEM((n - 1, traits, LANES), F32),
            pltpu.VMEM((chunks, traits, LANES), F32),
            pltpu.VMEM((traits, padded), F32),
            pltpu.VMEM((traits, padded), F32),
            pltpu.VMEM((traits, people), F32),
            pltpu.SemaphoreType.DMA((2,)),
            pltpu.SemaphoreType.DMA((2,)),
            pltpu.SemaphoreType.DMA((2,)),
            pltpu.SemaphoreType.DMA((2,)),
        ],
        compiler_params=pltpu.CompilerParams(
            collective_id=0, has_side_effects=True, vmem_limit_bytes=56 * 2**20
        ),
    )(genotypes, solution, residual, direction, ratio[:, None])


def solution(mesh):
    cols = P(None, ("cohort", "ind"))
    return jax.shard_map(
        functools.partial(per_device, mesh.shape["ind"]),
        mesh=mesh,
        in_specs=(P(("cohort", "ind"), None), cols, cols, cols, P("cohort")),
        out_specs=(cols, cols, cols),
        check_vma=False,
    )
```

```python
import functools

import jax
import jax.numpy as jnp
from jax import lax
from jax.experimental import pallas as pl
from jax.experimental.pallas import tpu as pltpu
from jax.sharding import PartitionSpec as P

ITERS = 8
LANES = 128
ROWS = 256
F32 = jnp.float32
BF16 = jnp.bfloat16


def split(value):
    high = value.astype(BF16)
    low = (value - high.astype(F32)).astype(BF16)
    return high, low


def product(rows, w_high, w_low):
    dims = (((1,), (0,)), ((), ()))
    count = rows.shape[0]
    high, low = split(rows)
    both = lax.dot_general(
        jnp.concatenate([high, low], axis=0), w_high, dims, preferred_element_type=F32
    )
    rest = lax.dot_general(high, w_low, dims, preferred_element_type=F32)
    return both[:count] + both[count:] + rest


def cg_kernel(
    n, snps, chunks,
    g_in, x_in, r_in, p_in, ratio_in,
    x_out, r_out, p_out,
    raw, gh, gl, th, tl, kh, kl, g_sem, first, part0, rs0, ag0, part, rs, ag, sums_ref, u_ref, image_ref, scalars, last,
    rs_send, rs_recv, ag_send, ag_recv,
):
    me = lax.axis_index("ind")
    people = x_in.shape[1]
    traits = x_in.shape[0]
    mine = (me * chunks + n - 1) // n
    is_owner = jnp.logical_and((mine * n) // chunks == me, mine < chunks)
    mine = jnp.minimum(mine, chunks - 1)

    rows = ROWS if people % ROWS == 0 else people
    steps = people // rows
    tail = (chunks - 1) * LANES

    def load(i):
        cut = pl.ds(pl.multiple_of(i * rows, rows), rows)
        return pltpu.make_async_copy(g_in.at[cut], raw.at[cut], g_sem.at[i])

    for i in range(steps):
        load(i).start()

    barrier = pltpu.get_barrier_semaphore()

    @pl.loop(1, n)
    def _(j):
        pl.semaphore_signal(
            barrier, inc=1, device_id={"ind": lax.rem(me + j, n)},
            device_id_type=pl.DeviceIdType.MESH,
        )

    pl.semaphore_wait(barrier, n - 1)

    def scatter_start(src, dst, which):
        for c in range(chunks):
            o = (c * n) // chunks

            @pl.when(me != o)
            def _():
                pltpu.make_async_remote_copy(
                    src_ref=src.at[c], dst_ref=dst.at[lax.rem(me - o - 1 + n, n)],
                    send_sem=rs_send.at[which], recv_sem=rs_recv.at[which],
                    device_id={"ind": o}, device_id_type=pl.DeviceIdType.MESH,
                ).start()

    def local(src, dst, send, recv):
        return pltpu.make_async_remote_copy(
            src_ref=src, dst_ref=dst, send_sem=send, recv_sem=recv,
            device_id={"ind": lax.rem(me + 1, n)},
            device_id_type=pl.DeviceIdType.MESH,
        )

    def sum_and_gather(src, buf, out, which):
        @pl.when(is_owner)
        def _():
            local(buf, buf, rs_send.at[which], rs_recv.at[which]).wait_recv()
            out[mine] = src[mine] + jnp.sum(buf[...], axis=0)

            @pl.loop(1, n)
            def _(j):
                pltpu.make_async_remote_copy(
                    src_ref=out.at[mine], dst_ref=out.at[mine],
                    send_sem=ag_send.at[which], recv_sem=ag_recv.at[which],
                    device_id={"ind": lax.rem(me + j, n)},
                    device_id_type=pl.DeviceIdType.MESH,
                ).start()

    def finish(src, buf, out, which):
        @pl.when(is_owner)
        def _():
            few = out.at[pl.ds(0, chunks - 1)]
            local(few, few, ag_send.at[which], ag_recv.at[which]).wait_recv()
            few = src.at[pl.ds(0, chunks - 1)]
            local(few, few, rs_send.at[which], rs_recv.at[which]).wait_send()
            local(buf, buf, ag_send.at[which], ag_recv.at[which]).wait_send()

        @pl.when(jnp.logical_not(is_owner))
        def _():
            local(out, out, ag_send.at[which], ag_recv.at[which]).wait_recv()
            local(src, src, rs_send.at[which], rs_recv.at[which]).wait_send()

    def put(dst, value):
        for c in range(chunks):
            dst[c] = value[:, c * LANES:(c + 1) * LANES]

    def whole(src):
        return jnp.concatenate([src[c] for c in range(chunks)], axis=1)

    wide = lax.broadcasted_iota(jnp.int32, (1, chunks * LANES), 1)
    real = wide < snps

    gh[:, tail:] = jnp.zeros((people, LANES), BF16)
    gl[:, tail:] = jnp.zeros((people, LANES), BF16)
    first[...] = jnp.zeros_like(first)

    @pl.loop(0, steps)
    def _(i):
        load(i).wait()
        cut = pl.ds(pl.multiple_of(i * rows, rows), rows)
        for c in range(chunks):
            lanes = slice(c * LANES, min((c + 1) * LANES, snps))
            high, low = split(raw[cut, lanes])
            gh[cut, lanes] = high
            gl[cut, lanes] = low
        both = jnp.concatenate([p_in[:, cut], r_in[:, cut]], axis=0)
        first[...] += product(both, gh[cut, :], gl[cut, :])

    put(part0, first[...])
    scatter_start(part0, rs0, 0)
    x_out[...] = x_in[...]
    r_out[...] = r_in[...]
    p_out[...] = p_in[...]

    @pl.loop(0, steps)
    def _(i):
        cut = pl.ds(pl.multiple_of(i * rows, rows), rows)
        th[:, cut] = gh[cut, :].T
        tl[:, cut] = gl[cut, :].T

    sum_and_gather(part0, rs0, ag0, 0)

    width = 2 * LANES
    for j in range(chunks // 2):
        lanes = slice(j * width, (j + 1) * width)
        top = (j + 1) * width
        block = (
            jnp.dot(th[:top], gh[:, lanes], preferred_element_type=F32)
            + jnp.dot(th[:top], gl[:, lanes], preferred_element_type=F32)
            + jnp.dot(tl[:top], gh[:, lanes], preferred_element_type=F32)
        )
        high, low = split(block)
        kh[:top, lanes] = high
        kl[:top, lanes] = low
        for i in range(j):
            under = slice(i * width, (i + 1) * width)
            kh[lanes, under] = high[under].T
            kl[lanes, under] = low[under].T

    finish(part0, rs0, ag0, 0)
    start = whole(ag0)
    sums_ref[...] = start[:traits]
    u_ref[...] = start[traits:]
    ratio = ratio_in[...]
    scale = 1.0 / snps
    half = people // 2

    def image_half(s, i):
        cut = pl.ds(i * half, half)
        image_ref[:, cut] = (
            product(s, th[:, cut], tl[:, cut]) * scale + ratio * p_out[:, cut]
        )

    @pl.loop(0, ITERS - 1)
    def _(step):
        s = sums_ref[...]
        t = product(s, kh[...], kl[...])
        r, p = r_out[...], p_out[...]
        rr = jnp.sum(r * r, axis=1, keepdims=True)
        rp = jnp.sum(r * p, axis=1, keepdims=True)
        pp = jnp.sum(p * p, axis=1, keepdims=True)
        t = t + jnp.where(
            wide == snps, rr,
            jnp.where(wide == snps + 1, rp, jnp.where(wide == snps + 2, pp, 0.0)),
        )
        put(part, t)
        scatter_start(part, rs, 1)
        image_half(s, 0)
        sum_and_gather(part, rs, ag, 1)
        image_half(s, 1)
        finish(part, rs, ag, 1)

        t = whole(ag)
        rr = t[:, snps:snps + 1]
        rp = t[:, snps + 1:snps + 2]
        pp = t[:, snps + 2:snps + 3]
        t = jnp.where(real, t, 0.0)
        u = u_ref[...]
        ss = jnp.sum(s * s, axis=1, keepdims=True) * scale
        us = jnp.sum(u * s, axis=1, keepdims=True) * scale
        ts = jnp.sum(t * s, axis=1, keepdims=True) * (scale * scale)
        alpha = rr / (ss + ratio * pp)
        cross = us + ratio * rp
        norm = ts + ratio * (2.0 * ss + ratio * pp)
        fresh = rr - alpha * (2.0 * cross - alpha * norm)
        beta = fresh / rr
        u = u - alpha * (t * scale + ratio * s)
        u_ref[...] = u
        sums_ref[...] = u + beta * s
        p = p_out[...]
        scalars[0] = jnp.broadcast_to(fresh, scalars.shape[1:])
        scalars[1] = jnp.broadcast_to(
            fresh + beta * (2.0 * (rp - rr) + beta * pp), scalars.shape[1:]
        )
        x_out[...] = x_out[...] + alpha * p
        r = r_out[...] - alpha * image_ref[...]
        r_out[...] = r
        p_out[...] = r + beta * p

    s = sums_ref[...]
    image_half(s, 0)
    image_half(s, 1)
    ss = jnp.sum(s * s, axis=1, keepdims=True) * scale
    alpha = scalars[0][:, :1] / (ss + ratio * scalars[1][:, :1])
    r, p = r_out[...], p_out[...]
    before = jnp.sum(r * r, axis=1, keepdims=True)
    r = r - alpha * image_ref[...]
    fresh = jnp.sum(r * r, axis=1, keepdims=True)
    lane = lax.broadcasted_iota(jnp.int32, scalars.shape[1:], 1)
    scalars[2] = jnp.where(lane == 0, before, fresh)

    @pl.loop(1, n)
    def _(j):
        pltpu.make_async_remote_copy(
            src_ref=scalars.at[2], dst_ref=last.at[n - 1 - j],
            send_sem=rs_send.at[2], recv_sem=rs_recv.at[2],
            device_id={"ind": lax.rem(me + j, n)},
            device_id_type=pl.DeviceIdType.MESH,
        ).start()

    r_out[...] = r
    x_out[...] = x_out[...] + alpha * p
    local(last, last, rs_send.at[2], rs_recv.at[2]).wait()
    both = scalars[2] + jnp.sum(last[...], axis=0)
    p_out[...] = r + (both[:, 1:2] / both[:, :1]) * p


def per_device(n, genotypes, solution, residual, direction, ratio):
    people, snps = genotypes.shape
    traits = solution.shape[0]
    chunks = -(-(snps + 3) // LANES)
    chunks += chunks % 2
    padded = chunks * LANES
    rows = ROWS if people % ROWS == 0 else people

    vmem = pl.BlockSpec(memory_space=pltpu.VMEM)
    shape = jax.ShapeDtypeStruct((traits, people), F32)
    return pl.pallas_call(
        functools.partial(cg_kernel, n, snps, chunks),
        out_shape=(shape, shape, shape),
        in_specs=[pl.BlockSpec(memory_space=pl.ANY)] + [vmem] * 4,
        out_specs=(vmem, vmem, vmem),
        scratch_shapes=[
            pltpu.VMEM((people, snps), F32),
            pltpu.VMEM((people, padded), BF16),
            pltpu.VMEM((people, padded), BF16),
            pltpu.VMEM((padded, people), BF16),
            pltpu.VMEM((padded, people), BF16),
            pltpu.VMEM((padded, padded), BF16),
            pltpu.VMEM((padded, padded), BF16),
            pltpu.SemaphoreType.DMA((people // rows,)),
            pltpu.VMEM((2 * traits, padded), F32),
            pltpu.VMEM((chunks, 2 * traits, LANES), F32),
            pltpu.VMEM((n - 1, 2 * traits, LANES), F32),
            pltpu.VMEM((chunks, 2 * traits, LANES), F32),
            pltpu.VMEM((chunks, traits, LANES), F32),
            pltpu.VMEM((n - 1, traits, LANES), F32),
            pltpu.VMEM((chunks, traits, LANES), F32),
            pltpu.VMEM((traits, padded), F32),
            pltpu.VMEM((traits, padded), F32),
            pltpu.VMEM((traits, people), F32),
            pltpu.VMEM((3, traits, LANES), F32),
            pltpu.VMEM((n - 1, traits, LANES), F32),
            pltpu.SemaphoreType.DMA((3,)),
            pltpu.SemaphoreType.DMA((3,)),
            pltpu.SemaphoreType.DMA((2,)),
            pltpu.SemaphoreType.DMA((2,)),
        ],
        compiler_params=pltpu.CompilerParams(
            collective_id=0, has_side_effects=True, vmem_limit_bytes=56 * 2**20
        ),
    )(genotypes, solution, residual, direction, ratio[:, None])


def solution(mesh):
    cols = P(None, ("cohort", "ind"))
    return jax.shard_map(
        functools.partial(per_device, mesh.shape["ind"]),
        mesh=mesh,
        in_specs=(P(("cohort", "ind"), None), cols, cols, cols, P("cohort")),
        out_specs=(cols, cols, cols),
        check_vma=False,
    )
```
